32 devices in a mesh: tok: 4 (over y, x), smp: 8 (over z, core).
Axes of the slice: x: 2, y: 2, z: 4, core: 2. Of those that a mesh axis runs over, the one named last changes fastest.
Arguments:
- row_table: float32 [8, 2048, 384], P('tok', 'smp'), may hold values from -6 to 6
- row_accum: float32 [8, 2048], P('tok', 'smp'), may hold values from 0.0001 to 0.01
- last_step: int32 [8, 2048], P('tok', 'smp'), may hold values from 0 to 47
- step_now: int32 [1], replicated, may hold values from 48 to 63
- row_ids: int32 [8, 8, 8, 2], P('tok', 'smp'), may hold values from 0 to 255, as said below
- row_counts: int32 [8, 8, 8], P('tok', 'smp'), may hold values from 1 to 2, as said below
- sample_slots: int32 [8, 2048], P(None, 'smp'), may hold values from 0 to 15, as said below
- labels: int32 [2048], P('smp'), may hold values 0 or 1
- up_weight: bfloat16 [384, 8, 1536], P('smp', 'tok'), may hold values from -0.3125 to 0.3125
- down_weight: bfloat16 [384, 8, 1536], P('smp', 'tok'), may hold values from -0.15625 to 0.15625
- out_weight: float32 [8, 384], P('tok'), may hold values from -0.3125 to 0.3125
Outputs:
- new_table: float32 [8, 2048, 384], P('tok', 'smp')
- new_accum: float32 [8, 2048], P('tok', 'smp')
- grad_down: float32 [384, 8, 1536], P('smp', 'tok')
- logits: float32 [2048], P('smp')
The draws below stay inside these ranges and needn't reach their ends.
Inputs may be any that keep to these rules, and one draw needn't show every extreme that they name: The first row_counts[t, o, g] entries of each list are distinct; later entries are padding; every token and owner has a list of 2 valid entries for some group. `row_ids`: row numbers within the owner's shard. `sample_slots`: each slot o * 2 + c names a valid entry c < row_counts[t, o, s // 256]. `last_step`: each row's last step is before step_now.
All inputs are finite; a program needn't handle non-finite values. No bound on the sum of `labels` on one device may be relied on, other than what follows from the above.
Results may differ from the reference program's by a relative error of at most 0.0021.
Values may be sent and summed in bfloat16 or wider, within the bound.
A program may use at most 64 MiB of HBM per device.

```python
import math
import jax
import jax.numpy as jnp
from jax import lax

D = 384
FF = 1536
TOKS = 8
BATCH = 256
CAP = 2
ROWS_DEV = 256
HEAD = 48
SAMPLES = 2048
ROWS = 2048
N_SMP = 8


def list_counts(key):
    base_key = jax.random.fold_in(key, 701)
    first_key = jax.random.fold_in(base_key, 1)
    second_key = jax.random.fold_in(base_key, 2)
    counts = jax.random.randint(first_key, (TOKS, N_SMP, N_SMP), 1, CAP + 1, dtype=jnp.int32)
    chosen = jax.random.randint(second_key, (TOKS, N_SMP), 0, N_SMP, dtype=jnp.int32)
    group_range = jnp.arange(N_SMP, dtype=jnp.int32)
    return jnp.where(group_range[None, None, :] == chosen[:, :, None], CAP, counts).astype(jnp.int32)


def draw_row_counts(key, part):
    return list_counts(key)


def draw_row_ids(key, part):
    base_key = jax.random.fold_in(key, 702)
    first_key = jax.random.fold_in(base_key, 1)
    second_key = jax.random.fold_in(base_key, 2)
    starts = jax.random.randint(first_key, (TOKS, N_SMP, N_SMP, 1), 0, ROWS_DEV, dtype=jnp.int32)
    strides = jax.random.randint(second_key, (TOKS, N_SMP, N_SMP, 1), 1, ROWS_DEV // CAP + 1, dtype=jnp.int32)
    offsets = jnp.arange(CAP, dtype=jnp.int32)[None, None, None, :]
    return ((starts + strides * offsets) % ROWS_DEV).astype(jnp.int32)


def draw_sample_slots(key, part):
    counts = list_counts(key)
    base_key = jax.random.fold_in(key, 703)
    first_key = jax.random.fold_in(base_key, 1)
    second_key = jax.random.fold_in(base_key, 2)
    owners = jax.random.randint(first_key, (TOKS, SAMPLES), 0, N_SMP, dtype=jnp.int32)
    groups = (jnp.arange(SAMPLES, dtype=jnp.int32) // BATCH)[None, :]
    tok_range = jnp.arange(TOKS, dtype=jnp.int32)[:, None]
    limits = counts[tok_range, owners, groups]
    within = jax.random.randint(second_key, (TOKS, SAMPLES), 0, limits, dtype=jnp.int32)
    return (owners * CAP + within).astype(jnp.int32)


def set_ends(result, own_key, least, largest):
    longest = result.shape.index(max(result.shape))
    spots = []
    for shift in (0, 1):
        where = [jax.random.randint(jax.random.fold_in(own_key, axis), (), 0, length) for axis, length in enumerate(result.shape)]
        where[longest] = (where[longest] + shift) % result.shape[longest]
        spots.append(tuple(where))
    return result.at[spots[0]].set(least).at[spots[1]].set(largest)


def levels(rng, shape, pieces, low, top_value):
    def one(position, shards_of):
        draws = jax.random.uniform(jax.random.fold_in(jax.random.fold_in(rng, 6), position), (shards_of,), jnp.float32, low / len(pieces), top_value / len(pieces))
        return jnp.repeat(jnp.exp(draws), shape[position] // shards_of).reshape((-1,) + (1,) * (len(shape) - position - 1))

    loudness = one(*pieces[0])
    for cut in pieces[1:]:
        loudness = loudness * one(*cut)
    return loudness


def normal_values(stream_key, shape, spread, limit, cuts=(), kind=jnp.bfloat16):
    array = jax.random.normal(stream_key, shape, jnp.float32) * spread
    if len(cuts) > 0:
        array = levels(stream_key, shape, cuts, -0.22, 0.18) * array
    return jnp.clip(array, min=-limit, max=limit).astype(kind)


def setup_inputs(seed: int = 0) -> dict:
    streams_of = jax.random.split(jax.random.key(seed), 12)
    return {
        "row_table": normal_values(streams_of[0], (TOKS, ROWS, D), 1.0, 6.0, ((0, 4), (1, 8)), jnp.float32),
        "row_accum": jnp.clip(jnp.exp(math.log(0.01) - 4.6051702 * jax.random.uniform(streams_of[1], (TOKS, ROWS), jnp.float32) ** levels(streams_of[1], (TOKS, ROWS), ((0, 4), (1, 8)), -0.2, 0.2)), 0.0001, 0.01),
        "last_step": set_ends(jax.random.randint(streams_of[2], (TOKS, ROWS), 0, 48), jax.random.fold_in(streams_of[2], 1), 0, 47).astype(jnp.int32),
        "step_now": jax.random.randint(streams_of[3], (1,), 48, 64).astype(jnp.int32),
        "row_ids": draw_row_ids(jax.random.fold_in(streams_of[11], 71), 0),
        "row_counts": draw_row_counts(jax.random.fold_in(streams_of[11], 71), 0),
        "sample_slots": draw_sample_slots(jax.random.fold_in(streams_of[11], 71), 0),
        "labels": set_ends((jax.random.randint(streams_of[7], (SAMPLES,), 0, 2) < 1).astype(jnp.int32), jax.random.fold_in(streams_of[7], 1), 0, 1),
        "up_weight": normal_values(streams_of[8], (D, TOKS, FF), D ** -0.5, 0.3125, ((0, 8), (1, 4))),
        "down_weight": normal_values(streams_of[9], (D, TOKS, FF), FF ** -0.5, 0.15625, ((0, 8), (1, 4))),
        "out_weight": normal_values(streams_of[10], (TOKS, D), D ** -0.5, 0.3125, ((0, 4),), jnp.float32),
    }


decay_log = math.log(0.98)
learn_rate = 0.2
norm_eps = 1e-05

def normalize(values):
    centre = lax.optimization_barrier(jnp.mean(values, axis=-1, keepdims=True))
    shifted = values - centre
    inverse = lax.rsqrt(lax.optimization_barrier(jnp.mean(shifted * shifted, axis=-1, keepdims=True)) + norm_eps)
    return (shifted * inverse, inverse)

def norm_back(grad_in, normed, inverse):
    first_mean = lax.optimization_barrier(jnp.mean(grad_in, axis=-1, keepdims=True))
    second = lax.optimization_barrier(jnp.mean(grad_in * normed, axis=-1, keepdims=True))
    return inverse * (grad_in - first_mean - normed * second)

def gelu_grad(preact):
    cumulative = 0.5 * (1.0 + lax.erf(preact * (1.0 / math.sqrt(2.0))))
    density = jnp.exp(-0.5 * preact * preact) * (1.0 / math.sqrt(2.0 * math.pi))
    return cumulative + preact * density

def swap_heads(values):
    return values.reshape(TOKS, SAMPLES, TOKS, HEAD).transpose(2, 1, 0, 3).reshape(TOKS, SAMPLES, D)

def reference(row_table, row_accum, last_step, step_now, row_ids, row_counts, sample_slots, labels, up_weight, down_weight, out_weight):
    highest = lax.Precision.HIGHEST
    tok_range = jnp.arange(TOKS).astype(jnp.int32)[:, None]
    elapsed = (step_now[0] - last_step).astype(jnp.float32)
    factor = jnp.exp(elapsed * decay_log)
    group_of = (jnp.arange(SAMPLES).astype(jnp.int32) // BATCH)[None, :]
    owner = sample_slots // CAP
    within = sample_slots % CAP
    local_id = row_ids[tok_range, owner, group_of, within]
    global_id = (owner * ROWS_DEV + local_id).astype(jnp.int32)
    own_rows = row_table[tok_range, global_id] * factor[tok_range, global_id][:, :, None]
    mixed_rows = swap_heads(own_rows)
    normed_in, inverse_in = normalize(own_rows + mixed_rows)
    input_bf = normed_in.astype(jnp.bfloat16)
    up_full = up_weight.astype(jnp.float32)
    down_full = down_weight.astype(jnp.float32)
    preact = jnp.einsum('tsd,dtf->tsf', input_bf.astype(jnp.float32), up_full, precision=highest)
    active = jax.nn.gelu(preact, approximate=False).astype(jnp.bfloat16)
    output = jnp.einsum('tsf,dtf->tsd', active.astype(jnp.float32), down_full, precision=highest)
    normed_out, inverse_out = normalize(normed_in + output)
    logits = jnp.einsum('tsd,td->s', normed_out, out_weight, precision=highest)
    dlogit = jax.nn.sigmoid(logits) - labels.astype(jnp.float32)
    grad_norm_out = dlogit[None, :, None] * out_weight[:, None, :]
    grad_sum = norm_back(grad_norm_out, normed_out, inverse_out)
    grad_out_bf = grad_sum.astype(jnp.bfloat16)
    grad_active = jnp.einsum('tsd,dtf->tsf', grad_out_bf.astype(jnp.float32), down_full, precision=highest)
    grad_pre = (grad_active * gelu_grad(preact)).astype(jnp.bfloat16)
    grad_normed = grad_sum + jnp.einsum('tsf,dtf->tsd', grad_pre.astype(jnp.float32), up_full, precision=highest)
    grad_mixed = norm_back(grad_normed, normed_in, inverse_in)
    grad_rows_all = grad_mixed + swap_heads(grad_mixed)
    row_grads = jnp.zeros((TOKS, ROWS, D), jnp.float32).at[tok_range, global_id].add(grad_rows_all)
    tok_four = jnp.arange(TOKS).astype(jnp.int32)[:, None, None, None]
    valid_slot = (jnp.arange(CAP).astype(jnp.int32)[None, None, None, :] < row_counts[:, :, :, None]).astype(jnp.float32)
    list_global = (jnp.arange(N_SMP).astype(jnp.int32)[None, :, None, None] * ROWS_DEV + row_ids).astype(jnp.int32)
    hits = jnp.zeros((TOKS, ROWS), jnp.float32).at[tok_four, list_global].add(valid_slot)
    touched = hits > 0.0
    new_accum = row_accum + lax.optimization_barrier(jnp.mean(row_grads * row_grads, axis=2))
    updated = row_table * factor[:, :, None] - learn_rate * row_grads * lax.rsqrt(new_accum)[:, :, None]
    new_table = jnp.where(touched[:, :, None], updated, row_table)
    grad_down = jnp.einsum('tsd,tsf->dtf', grad_out_bf.astype(jnp.float32), active.astype(jnp.float32), precision=highest)
    return (new_table, new_accum, grad_down, logits)
```

```python
import functools
import math

import jax
import jax.numpy as jnp
from jax import lax
from jax.experimental import pallas as pl
from jax.experimental.pallas import tpu as pltpu
from jax.sharding import PartitionSpec as P

decay_log = math.log(0.98)
learn_rate = 0.2
norm_eps = 1e-05
MESH = pl.DeviceIdType.MESH
VMEM = pltpu.VMEM


def normalize(values):
    centre = jnp.mean(values, axis=-1, keepdims=True)
    shifted = values - centre
    inverse = lax.rsqrt(jnp.mean(shifted * shifted, axis=-1, keepdims=True) + norm_eps)
    return (shifted * inverse, inverse)


def norm_back(grad_in, normed, inverse):
    first_mean = jnp.mean(grad_in, axis=-1, keepdims=True)
    second = jnp.mean(grad_in * normed, axis=-1, keepdims=True)
    return inverse * (grad_in - first_mean - normed * second)


def gelu_grad(preact):
    cumulative = 0.5 * (1.0 + lax.erf(preact * (1.0 / math.sqrt(2.0))))
    density = jnp.exp(-0.5 * preact * preact) * (1.0 / math.sqrt(2.0 * math.pi))
    return cumulative + preact * density


def greet(axes):
    barrier = pltpu.get_barrier_semaphore()
    total = 0
    for name, size in axes:
        me = lax.axis_index(name)
        for k in range(1, size):
            pl.semaphore_signal(barrier, inc=1, device_id={name: lax.rem(me + k, size)}, device_id_type=MESH)
        total += size - 1
    pl.semaphore_wait(barrier, total)


def send_all(name, size, source, target, send_sem, recv_sem):
    me = lax.axis_index(name)
    copies = []
    for k in range(1, size):
        peer = lax.rem(me + k, size)
        copy = pltpu.make_async_remote_copy(
            src_ref=source(peer),
            dst_ref=target,
            send_sem=send_sem.at[k],
            recv_sem=recv_sem.at[k],
            device_id={name: peer},
            device_id_type=MESH,
        )
        copy.start()
        copies.append(copy)
    return copies


def lists_kernel(n_tok, n_smp, x_ref, y_ref, send_a, recv_a, send_b, recv_b):
    tok, smp = lax.axis_index("tok"), lax.axis_index("smp")
    greet((("smp", n_smp), ("tok", n_tok)))
    copies = send_all("smp", n_smp, lambda p: x_ref.at[p], y_ref.at[tok, smp], send_a, recv_a)
    y_ref[tok, smp] = x_ref[smp]
    for copy in copies:
        copy.wait()
    for copy in send_all("tok", n_tok, lambda p: y_ref.at[tok], y_ref.at[tok], send_b, recv_b):
        copy.wait()


def grads_kernel(n_tok, n_smp, s_ref, y_ref, landed, total, send_a, recv_a, send_b, recv_b):
    tok, smp = lax.axis_index("tok"), lax.axis_index("smp")
    greet((("smp", n_smp), ("tok", n_tok)))
    copies = send_all("tok", n_tok, lambda p: s_ref.at[p], landed.at[tok], send_a, recv_a)
    landed[tok] = s_ref[tok]
    for copy in copies:
        copy.wait()
    total[...] = jnp.sum(landed[...], axis=0)
    copies = send_all("smp", n_smp, lambda p: total.at[p], y_ref.at[smp], send_b, recv_b)
    y_ref[smp] = total[smp]
    for copy in copies:
        copy.wait()


def logits_kernel(n_tok, x_ref, y_ref, landed, send_sem, recv_sem):
    tok = lax.axis_index("tok")
    greet((("tok", n_tok),))
    copies = send_all("tok", n_tok, lambda p: x_ref, landed.at[tok], send_sem, recv_sem)
    landed[tok] = x_ref[...]
    for copy in copies:
        copy.wait()
    y_ref[...] = jnp.sum(landed[...], axis=0)


def call(kernel, operand, out_shape, scratch, sems, ident):
    return pl.pallas_call(
        kernel,
        out_shape=jax.ShapeDtypeStruct(out_shape, jnp.float32),
        in_specs=[pl.BlockSpec(memory_space=VMEM)],
        out_specs=pl.BlockSpec(memory_space=VMEM),
        scratch_shapes=[VMEM(s, jnp.float32) for s in scratch]
        + [pltpu.SemaphoreType.DMA((n,)) for n in sems],
        compiler_params=pltpu.CompilerParams(
            collective_id=ident, has_side_effects=True, vmem_limit_bytes=24 << 20
        ),
        cost_estimate=pl.CostEstimate(flops=0, bytes_accessed=30_000_000, transcendentals=0),
    )(operand)


def on_device(
    n_tok,
    n_smp,
    row_table,
    row_accum,
    last_step,
    step_now,
    row_ids,
    row_counts,
    sample_slots,
    labels,
    up_weight,
    down_weight,
    out_weight,
):
    highest = lax.Precision.HIGHEST
    local_toks, shard_rows, width = row_table.shape
    groups, capacity = row_ids.shape[2:]
    batch = labels.shape[0]
    toks = sample_slots.shape[0]
    head = width // toks
    rows = local_toks * capacity
    flat = n_tok * n_smp * rows
    tok, smp = lax.axis_index("tok"), lax.axis_index("smp")

    up_full = lax.all_gather(up_weight, "smp", axis=0, tiled=True)
    down_full = lax.all_gather(down_weight, "smp", axis=0, tiled=True)

    factor = jnp.exp((step_now[0] - last_step).astype(jnp.float32) * decay_log)
    ids = row_ids[:, 0].transpose(1, 0, 2)
    valid = jnp.arange(capacity)[None, None, :] < row_counts[:, 0].T[:, :, None]
    pick = ids[..., None] == jnp.arange(shard_rows)
    looked = jnp.einsum(
        "gjcr,jrd->gjcd", pick.astype(jnp.float32), row_table * factor[:, :, None], precision=highest
    ).reshape(groups, rows, width)
    lists = call(
        functools.partial(lists_kernel, n_tok, n_smp),
        looked,
        (n_tok, n_smp, rows, width),
        [],
        [n_smp, n_smp, n_tok, n_tok],
        1,
    ).reshape(flat, width)

    place = jnp.arange(n_smp)[:, None] * capacity + jnp.arange(capacity)
    slots = sample_slots.reshape(n_tok, 1, local_toks, 1, batch)
    hits = (slots == place[None, :, None, :, None]).astype(jnp.float32).reshape(flat, batch)
    number = jnp.arange(flat)
    token = number // (n_smp * rows) * local_toks + number % rows // capacity
    block = token[:, None] == (jnp.arange(width) // head)[None, :]
    mine = [(token == tok * local_toks + j)[:, None] for j in range(local_toks)]

    gathered = []
    for j in range(local_toks):
        part = lax.dynamic_slice_in_dim(lists, (tok * local_toks + j) * head, head, 1)
        spread = jnp.where(block, jnp.tile(part, (1, toks)), 0.0)
        gathered.append(spread + jnp.where(mine[j], lists, 0.0))
    summed = jnp.einsum("kb,jkd->jbd", hits, jnp.stack(gathered), precision=highest)
    normed_in, inverse_in = normalize(summed)
    input_bf = normed_in.astype(jnp.bfloat16)
    preact = jnp.einsum("jbd,djf->jbf", input_bf, up_full, preferred_element_type=jnp.float32)
    active = jax.nn.gelu(preact, approximate=False).astype(jnp.bfloat16)
    output = jnp.einsum("jbf,djf->jbd", active, down_full, preferred_element_type=jnp.float32)
    normed_out, inverse_out = normalize(normed_in + output)
    partial_logit = jnp.sum(normed_out * out_weight[:, None, :], axis=(0, 2))
    logits = call(
        functools.partial(logits_kernel, n_tok),
        partial_logit.reshape(1, batch),
        (1, batch),
        [(n_tok, 1, batch)],
        [n_tok, n_tok],
        2,
    ).reshape(batch)
    dlogit = jax.nn.sigmoid(logits) - labels.astype(jnp.float32)
    grad_sum = norm_back(dlogit[None, :, None] * out_weight[:, None, :], normed_out, inverse_out)
    grad_out_bf = grad_sum.astype(jnp.bfloat16)

    near = 2 if n_smp % 2 == 0 else 1
    far = n_smp // near
    partial = jnp.einsum("jbd,jbf->jdf", grad_out_bf, active, preferred_element_type=jnp.float32)
    partial = partial.reshape(local_toks, far, near, width // n_smp, -1)
    z, core = smp // near, smp % near
    pair = lax.dynamic_index_in_dim(partial, core, 2, keepdims=False)
    if near == 2:
        other = lax.dynamic_index_in_dim(partial, 1 - core, 2, keepdims=False)
        pair = pair + lax.ppermute(other, "smp", [(i, i ^ 1) for i in range(n_smp)])
    def far_sums(pair):
        grad_down = lax.dynamic_index_in_dim(pair, z, 1, keepdims=False)
        flip = far & (far - 1) == 0
        for k in range(far - 1, 0, -1):
            partner = z ^ k if flip else (z + k) % far
            part = lax.dynamic_index_in_dim(pair, partner, 1, keepdims=False)
            if not (flip and k == 1):
                part = part.astype(jnp.bfloat16)
            route = [(i, i ^ (k * near) if flip else (i + k * near) % n_smp) for i in range(n_smp)]
            grad_down = grad_down + lax.ppermute(part, "smp", route).astype(jnp.float32)
        return grad_down.transpose(1, 0, 2)

    grad_active = jnp.einsum(
        "jbd,djf->jbf", grad_out_bf, down_full, preferred_element_type=jnp.float32
    )
    grad_pre = (grad_active * gelu_grad(preact)).astype(jnp.bfloat16)
    grad_normed = grad_sum + jnp.einsum(
        "jbf,djf->jbd", grad_pre, up_full, preferred_element_type=jnp.float32
    )
    grad_mixed = norm_back(grad_normed, normed_in, inverse_in)
    pair, grad_mixed = lax.optimization_barrier((pair, grad_mixed))
    grad_down = far_sums(pair)

    sums = jnp.einsum("kb,jbd->jkd", hits, grad_mixed, precision=highest)
    sent = jnp.zeros((flat, width), jnp.float32)
    for j in range(local_toks):
        own_head = (jnp.arange(width) // head == tok * local_toks + j)[None, :]
        heads = jnp.where(block, sums[j], 0.0).reshape(flat, toks, head).sum(axis=1)
        sent = sent + jnp.where(own_head, jnp.tile(heads, (1, toks)), 0.0)
        sent = sent + jnp.where(mine[j], sums[j], 0.0)
    back = call(
        functools.partial(grads_kernel, n_tok, n_smp),
        sent.reshape(n_tok, n_smp, rows, width),
        (n_smp, rows, width),
        [(n_tok, n_smp, rows, width), (n_smp, rows, width)],
        [n_tok, n_tok, n_smp, n_smp],
        3,
    ).reshape(groups, local_toks, capacity, width)

    taken = (pick & valid[..., None]).astype(jnp.float32)
    row_grads = jnp.einsum("gjcr,gjcd->jrd", taken, back, precision=highest)
    touched = jnp.sum(taken, axis=(0, 2)) > 0.0
    new_accum = row_accum + jnp.mean(row_grads * row_grads, axis=2)
    updated = row_table * factor[:, :, None] - learn_rate * row_grads * lax.rsqrt(new_accum)[:, :, None]
    new_table = jnp.where(touched[:, :, None], updated, row_table)
    return (new_table, new_accum, grad_down, logits)


def solution(mesh):
    return jax.shard_map(
        functools.partial(on_device, mesh.shape["tok"], mesh.shape["smp"]),
        mesh=mesh,
        in_specs=(
            P("tok", "smp", None),
            P("tok", "smp"),
            P("tok", "smp"),
            P(),
            P("tok", "smp", None, None),
            P("tok", "smp", None),
            P(None, "smp"),
            P("smp"),
            P("smp", "tok", None),
            P("smp", "tok", None),
            P("tok", None),
        ),
        out_specs=(P("tok", "smp", None), P("tok", "smp"), P("smp", "tok", None), P("smp")),
        check_vma=False,
    )
```

```python
import functools
import math

import jax
import jax.numpy as jnp
from jax import lax
from jax.experimental import pallas as pl
from jax.experimental.pallas import tpu as pltpu
from jax.sharding import PartitionSpec as P

decay_log = math.log(0.98)
learn_rate = 0.2
norm_eps = 1e-05
MESH = pl.DeviceIdType.MESH
VMEM = pltpu.VMEM


def normalize(values):
    centre = jnp.mean(values, axis=-1, keepdims=True)
    shifted = values - centre
    inverse = lax.rsqrt(jnp.mean(shifted * shifted, axis=-1, keepdims=True) + norm_eps)
    return (shifted * inverse, inverse)


def norm_back(grad_in, normed, inverse):
    first_mean = jnp.mean(grad_in, axis=-1, keepdims=True)
    second = jnp.mean(grad_in * normed, axis=-1, keepdims=True)
    return inverse * (grad_in - first_mean - normed * second)


def gelu_grad(preact):
    cumulative = 0.5 * (1.0 + lax.erf(preact * (1.0 / math.sqrt(2.0))))
    density = jnp.exp(-0.5 * preact * preact) * (1.0 / math.sqrt(2.0 * math.pi))
    return cumulative + preact * density


def greet(axes):
    barrier = pltpu.get_barrier_semaphore()
    total = 0
    for name, size in axes:
        me = lax.axis_index(name)
        for k in range(1, size):
            pl.semaphore_signal(barrier, inc=1, device_id={name: lax.rem(me + k, size)}, device_id_type=MESH)
        total += size - 1
    pl.semaphore_wait(barrier, total)


def send_all(name, size, source, target, send_sem, recv_sem):
    me = lax.axis_index(name)
    copies = []
    for k in range(1, size):
        peer = lax.rem(me + k, size)
        copy = pltpu.make_async_remote_copy(
            src_ref=source(peer),
            dst_ref=target,
            send_sem=send_sem.at[k],
            recv_sem=recv_sem.at[k],
            device_id={name: peer},
            device_id_type=MESH,
        )
        copy.start()
        copies.append(copy)
    return copies


def lists_kernel(
    n_tok, n_smp, near, x_ref, w_ref, y_ref, up_ref, send_a, recv_a, send_b, recv_b, hop_send, hop_recv, swap_send, swap_recv
):
    tok, smp = lax.axis_index("tok"), lax.axis_index("smp")
    z, core = smp // near, lax.rem(smp, near)
    far = n_smp // near
    local_toks = w_ref.shape[0]
    chunks = [(j, way) for j in range(local_toks) for way in (0, 1)]

    def hop(j, way, step):
        sign = 1 - 2 * way
        block = up_ref.at[j, (z - sign * (step - 1) + far) % far * near + core]
        return pltpu.make_async_remote_copy(
            src_ref=block,
            dst_ref=block,
            send_sem=hop_send.at[j, way, step],
            recv_sem=hop_recv.at[j, way, step],
            device_id={"smp": (z + sign + far) % far * near + core},
            device_id_type=MESH,
        )

    def leaves(way, step):
        return (z >= step - 1) & (z + 1 < far) if way == 0 else (z + step - 1 < far) & (z >= 1)

    def lands(way, step):
        return z >= step if way == 0 else z + step < far

    def swap(j, position):
        block = up_ref.at[j, position * near + core]
        return pltpu.make_async_remote_copy(
            src_ref=block,
            dst_ref=block,
            send_sem=swap_send.at[j, position],
            recv_sem=swap_recv.at[j, position],
            device_id={"smp": z * near + near - 1 - core},
            device_id_type=MESH,
        )

    def arrived(j, way, step):
        sign = 1 - 2 * way
        block = up_ref.at[j, (z - sign * step + far) % far * near + core]
        pltpu.make_async_remote_copy(
            src_ref=block,
            dst_ref=block,
            send_sem=hop_send.at[j, way, step],
            recv_sem=hop_recv.at[j, way, step],
            device_id={"smp": (z + sign + far) % far * near + core},
            device_id_type=MESH,
        ).wait_recv()

    for j in range(local_toks):
        up_ref[j, smp] = w_ref[j]
    greet((("smp", n_smp), ("tok", n_tok)))
    copies = send_all("smp", n_smp, lambda p: x_ref.at[p], y_ref.at[tok, smp], send_a, recv_a)
    for j, way in chunks:
        pl.when(leaves(way, 1))(lambda j=j, way=way: hop(j, way, 1).start())
    if near == 2:
        for j in range(local_toks):
            swap(j, z).start()
    y_ref[tok, smp] = x_ref[smp]
    for copy in copies:
        copy.wait()
    copies = send_all("tok", n_tok, lambda p: y_ref.at[tok], y_ref.at[tok], send_b, recv_b)

    def relay(step, carry):
        for j, way in chunks:

            @pl.when(lands(way, step))
            def _(j=j, way=way):
                arrived(j, way, step)
                pl.when((step + 1 < far) & leaves(way, step + 1))(lambda: hop(j, way, step + 1).start())
                if near == 2:
                    swap(j, z - step if way == 0 else z + step).start()

        return carry

    lax.fori_loop(1, far, relay, 0)

    def finish(step, carry):
        for j, way in chunks:
            pl.when(leaves(way, step))(lambda j=j, way=way: hop(j, way, step).wait_send())
        return carry

    lax.fori_loop(1, far, finish, 0)
    if near == 2:

        def swapped(position, carry):
            for j in range(local_toks):
                swap(j, position).wait()
            return carry

        lax.fori_loop(0, far, swapped, 0)
    for copy in copies:
        copy.wait()


def grads_kernel(n_tok, n_smp, s_ref, y_ref, landed, total, send_a, recv_a, send_b, recv_b):
    tok, smp = lax.axis_index("tok"), lax.axis_index("smp")
    greet((("smp", n_smp), ("tok", n_tok)))
    copies = send_all("tok", n_tok, lambda p: s_ref.at[p], landed.at[tok], send_a, recv_a)
    landed[tok] = s_ref[tok]
    for copy in copies:
        copy.wait()
    total[...] = jnp.sum(landed[...], axis=0)
    copies = send_all("smp", n_smp, lambda p: total.at[p], y_ref.at[smp], send_b, recv_b)
    y_ref[smp] = total[smp]
    for copy in copies:
        copy.wait()


def logits_kernel(n_tok, x_ref, y_ref, landed, send_sem, recv_sem):
    tok = lax.axis_index("tok")
    greet((("tok", n_tok),))
    copies = send_all("tok", n_tok, lambda p: x_ref, landed.at[tok], send_sem, recv_sem)
    landed[tok] = x_ref[...]
    for copy in copies:
        copy.wait()
    y_ref[...] = jnp.sum(landed[...], axis=0)


def call(kernel, operand, out_shape, scratch, sems, ident):
    return pl.pallas_call(
        kernel,
        out_shape=jax.ShapeDtypeStruct(out_shape, jnp.float32),
        in_specs=[pl.BlockSpec(memory_space=VMEM)],
        out_specs=pl.BlockSpec(memory_space=VMEM),
        scratch_shapes=[VMEM(s, jnp.float32) for s in scratch]
        + [pltpu.SemaphoreType.DMA((n,)) for n in sems],
        compiler_params=pltpu.CompilerParams(
            collective_id=ident, has_side_effects=True, vmem_limit_bytes=24 << 20
        ),
        cost_estimate=pl.CostEstimate(flops=0, bytes_accessed=30_000_000, transcendentals=0),
    )(operand)


def on_device(
    n_tok,
    n_smp,
    row_table,
    row_accum,
    last_step,
    step_now,
    row_ids,
    row_counts,
    sample_slots,
    labels,
    up_weight,
    down_weight,
    out_weight,
):
    highest = lax.Precision.HIGHEST
    local_toks, shard_rows, width = row_table.shape
    groups, capacity = row_ids.shape[2:]
    batch = labels.shape[0]
    toks = sample_slots.shape[0]
    head = width // toks
    rows = local_toks * capacity
    flat = n_tok * n_smp * rows
    tok, smp = lax.axis_index("tok"), lax.axis_index("smp")

    down_full = lax.all_gather(down_weight, "smp", axis=0, tiled=True)

    factor = jnp.exp((step_now[0] - last_step).astype(jnp.float32) * decay_log)
    ids = row_ids[:, 0].transpose(1, 0, 2)
    valid = jnp.arange(capacity)[None, None, :] < row_counts[:, 0].T[:, :, None]
    pick = ids[..., None] == jnp.arange(shard_rows)
    looked = jnp.einsum(
        "gjcr,jrd->gjcd", pick.astype(jnp.float32), row_table * factor[:, :, None], precision=highest
    ).reshape(groups, rows, width)
    near = 2 if n_smp % 2 == 0 else 1
    far = n_smp // near
    up_blocks = up_weight.transpose(1, 0, 2)
    hops = (local_toks, 2, far)
    lists, up_full = pl.pallas_call(
        functools.partial(lists_kernel, n_tok, n_smp, near),
        out_shape=(
            jax.ShapeDtypeStruct((n_tok, n_smp, rows, width), jnp.float32),
            jax.ShapeDtypeStruct((local_toks, n_smp) + up_blocks.shape[1:], jnp.bfloat16),
        ),
        in_specs=[pl.BlockSpec(memory_space=VMEM)] * 2,
        out_specs=(pl.BlockSpec(memory_space=VMEM),) * 2,
        scratch_shapes=[pltpu.SemaphoreType.DMA((n,)) for n in (n_smp, n_smp, n_tok, n_tok)]
        + [pltpu.SemaphoreType.DMA(n) for n in (hops, hops, (local_toks, far), (local_toks, far))],
        compiler_params=pltpu.CompilerParams(
            collective_id=1, has_side_effects=True, vmem_limit_bytes=24 << 20
        ),
        cost_estimate=pl.CostEstimate(flops=0, bytes_accessed=60_000_000, transcendentals=0),
    )(looked, up_blocks)
    lists = lists.reshape(flat, width)
    up_full = up_full.reshape(local_toks, width, -1)

    place = jnp.arange(n_smp)[:, None] * capacity + jnp.arange(capacity)
    slots = sample_slots.reshape(n_tok, 1, local_toks, 1, batch)
    hits = (slots == place[None, :, None, :, None]).astype(jnp.float32).reshape(flat, batch)
    number = jnp.arange(flat)
    token = number // (n_smp * rows) * local_toks + number % rows // capacity
    block = token[:, None] == (jnp.arange(width) // head)[None, :]
    mine = [(token == tok * local_toks + j)[:, None] for j in range(local_toks)]

    gathered = []
    for j in range(local_toks):
        part = lax.dynamic_slice_in_dim(lists, (tok * local_toks + j) * head, head, 1)
        spread = jnp.where(block, jnp.tile(part, (1, toks)), 0.0)
        gathered.append(spread + jnp.where(mine[j], lists, 0.0))
    summed = jnp.einsum("kb,jkd->jbd", hits, jnp.stack(gathered), precision=highest)
    normed_in, inverse_in = normalize(summed)
    input_bf = normed_in.astype(jnp.bfloat16)
    preact = jnp.einsum("jbd,jdf->jbf", input_bf, up_full, preferred_element_type=jnp.float32)
    active = jax.nn.gelu(preact, approximate=False).astype(jnp.bfloat16)
    output = jnp.einsum("jbf,djf->jbd", active, down_full, preferred_element_type=jnp.float32)
    normed_out, inverse_out = normalize(normed_in + output)
    partial_logit = jnp.sum(normed_out * out_weight[:, None, :], axis=(0, 2))
    logits = call(
        functools.partial(logits_kernel, n_tok),
        partial_logit.reshape(1, batch),
        (1, batch),
        [(n_tok, 1, batch)],
        [n_tok, n_tok],
        2,
    ).reshape(batch)
    dlogit = jax.nn.sigmoid(logits) - labels.astype(jnp.float32)
    grad_sum = norm_back(dlogit[None, :, None] * out_weight[:, None, :], normed_out, inverse_out)
    grad_out_bf = grad_sum.astype(jnp.bfloat16)

    z, core = smp // near, smp % near
    pairs = []
    for j in range(local_toks):
        partial = jnp.einsum("bd,bf->df", grad_out_bf[j], active[j], preferred_element_type=jnp.float32)
        partial = partial.reshape(far, near, width // n_smp, -1)
        pair = lax.dynamic_index_in_dim(partial, core, 1, keepdims=False)
        if near == 2:
            other = lax.dynamic_index_in_dim(partial, 1 - core, 1, keepdims=False)
            pair = pair + lax.ppermute(other, "smp", [(i, i ^ 1) for i in range(n_smp)])
        pairs.append(pair)

    def far_sums(pair):
        grad_down = lax.dynamic_index_in_dim(pair, z, 0, keepdims=False)
        flip = far & (far - 1) == 0
        for k in range(far - 1, 0, -1):
            partner = z ^ k if flip else (z + k) % far
            part = lax.dynamic_index_in_dim(pair, partner, 0, keepdims=False)
            if not (flip and k == 1):
                part = part.astype(jnp.bfloat16)
            route = [(i, i ^ (k * near) if flip else (i + k * near) % n_smp) for i in range(n_smp)]
            grad_down = grad_down + lax.ppermute(part, "smp", route).astype(jnp.float32)
        return grad_down

    grad_active = jnp.einsum(
        "jbd,djf->jbf", grad_out_bf, down_full, preferred_element_type=jnp.float32
    )
    grad_pre = (grad_active * gelu_grad(preact)).astype(jnp.bfloat16)
    grad_normed = grad_sum + jnp.einsum(
        "jbf,jdf->jbd", grad_pre, up_full, preferred_element_type=jnp.float32
    )
    grad_mixed = norm_back(grad_normed, normed_in, inverse_in)
    pairs, grad_mixed = lax.optimization_barrier((pairs, grad_mixed))
    grad_down = jnp.stack([far_sums(pair) for pair in pairs], axis=1)

    sums = jnp.einsum("kb,jbd->jkd", hits, grad_mixed, precision=highest)
    sent = jnp.zeros((flat, width), jnp.float32)
    for j in range(local_toks):
        own_head = (jnp.arange(width) // head == tok * local_toks + j)[None, :]
        heads = jnp.where(block, sums[j], 0.0).reshape(flat, toks, head).sum(axis=1)
        sent = sent + jnp.where(own_head, jnp.tile(heads, (1, toks)), 0.0)
        sent = sent + jnp.where(mine[j], sums[j], 0.0)
    back = call(
        functools.partial(grads_kernel, n_tok, n_smp),
        sent.reshape(n_tok, n_smp, rows, width),
        (n_smp, rows, width),
        [(n_tok, n_smp, rows, width), (n_smp, rows, width)],
        [n_tok, n_tok, n_smp, n_smp],
        3,
    ).reshape(groups, local_toks, capacity, width)

    taken = (pick & valid[..., None]).astype(jnp.float32)
    row_grads = jnp.einsum("gjcr,gjcd->jrd", taken, back, precision=highest)
    touched = jnp.sum(taken, axis=(0, 2)) > 0.0
    new_accum = row_accum + jnp.mean(row_grads * row_grads, axis=2)
    updated = row_table * factor[:, :, None] - learn_rate * row_grads * lax.rsqrt(new_accum)[:, :, None]
    new_table = jnp.where(touched[:, :, None], updated, row_table)
    return (new_table, new_accum, grad_down, logits)


def solution(mesh):
    return jax.shard_map(
        functools.partial(on_device, mesh.shape["tok"], mesh.shape["smp"]),
        mesh=mesh,
        in_specs=(
            P("tok", "smp", None),
            P("tok", "smp"),
            P("tok", "smp"),
            P(),
            P("tok", "smp", None, None),
            P("tok", "smp", None),
            P(None, "smp"),
            P("smp"),
            P("smp", "tok", None),
            P("smp", "tok", None),
            P("tok", None),
        ),
        out_specs=(P("tok", "smp", None), P("tok", "smp"), P("smp", "tok", None), P("smp")),
        check_vma=False,
    )
```

```python
import functools
import math

import jax
import jax.numpy as jnp
from jax import lax
from jax.experimental import pallas as pl
from jax.experimental.pallas import tpu as pltpu
from jax.sharding import PartitionSpec as P

decay_log = math.log(0.98)
learn_rate = 0.2
norm_eps = 1e-05
MESH = pl.DeviceIdType.MESH
VMEM = pltpu.VMEM


def normalize(values):
    centre = jnp.mean(values, axis=-1, keepdims=True)
    shifted = values - centre
    inverse = lax.rsqrt(jnp.mean(shifted * shifted, axis=-1, keepdims=True) + norm_eps)
    return (shifted * inverse, inverse)


def norm_back(grad_in, normed, inverse):
    first_mean = jnp.mean(grad_in, axis=-1, keepdims=True)
    second = jnp.mean(grad_in * normed, axis=-1, keepdims=True)
    return inverse * (grad_in - first_mean - normed * second)


def gelu_grad(preact):
    cumulative = 0.5 * (1.0 + lax.erf(preact * (1.0 / math.sqrt(2.0))))
    density = jnp.exp(-0.5 * preact * preact) * (1.0 / math.sqrt(2.0 * math.pi))
    return cumulative + preact * density


def greet(axes):
    barrier = pltpu.get_barrier_semaphore()
    total = 0
    for name, size in axes:
        me = lax.axis_index(name)
        for k in range(1, size):
            pl.semaphore_signal(barrier, inc=1, device_id={name: lax.rem(me + k, size)}, device_id_type=MESH)
        total += size - 1
    pl.semaphore_wait(barrier, total)


def send_all(name, size, source, target, send_sem, recv_sem):
    me = lax.axis_index(name)
    copies = []
    for k in range(1, size):
        peer = lax.rem(me + k, size)
        copy = pltpu.make_async_remote_copy(
            src_ref=source(peer),
            dst_ref=target,
            send_sem=send_sem.at[k],
            recv_sem=recv_sem.at[k],
            device_id={name: peer},
            device_id_type=MESH,
        )
        copy.start()
        copies.append(copy)
    return copies


def lists_kernel(
    n_tok, n_smp, near, x_ref, w_ref, y_ref, up_ref, send_a, recv_a, send_b, recv_b, hop_send, hop_recv, swap_send, swap_recv
):
    tok, smp = lax.axis_index("tok"), lax.axis_index("smp")
    z, core = smp // near, lax.rem(smp, near)
    far = n_smp // near
    local_toks = w_ref.shape[0]
    chunks = [(j, way) for j in range(local_toks) for way in (0, 1)]

    def hop(j, way, step):
        sign = 1 - 2 * way
        block = up_ref.at[j, (z - sign * (step - 1) + far) % far * near + core]
        return pltpu.make_async_remote_copy(
            src_ref=block,
            dst_ref=block,
            send_sem=hop_send.at[j, way, step],
            recv_sem=hop_recv.at[j, way, step],
            device_id={"smp": (z + sign + far) % far * near + core},
            device_id_type=MESH,
        )

    def leaves(way, step):
        return (z >= step - 1) & (z + 1 < far) if way == 0 else (z + step - 1 < far) & (z >= 1)

    def lands(way, step):
        return z >= step if way == 0 else z + step < far

    def swap(j, position):
        block = up_ref.at[j, position * near + core]
        return pltpu.make_async_remote_copy(
            src_ref=block,
            dst_ref=block,
            send_sem=swap_send.at[j, position],
            recv_sem=swap_recv.at[j, position],
            device_id={"smp": z * near + near - 1 - core},
            device_id_type=MESH,
        )

    def arrived(j, way, step):
        sign = 1 - 2 * way
        block = up_ref.at[j, (z - sign * step + far) % far * near + core]
        pltpu.make_async_remote_copy(
            src_ref=block,
            dst_ref=block,
            send_sem=hop_send.at[j, way, step],
            recv_sem=hop_recv.at[j, way, step],
            device_id={"smp": (z + sign + far) % far * near + core},
            device_id_type=MESH,
        ).wait_recv()

    for j in range(local_toks):
        up_ref[j, smp] = w_ref[j]
    greet((("smp", n_smp), ("tok", n_tok)))
    copies = send_all("smp", n_smp, lambda p: x_ref.at[p], y_ref.at[tok, smp], send_a, recv_a)
    for j, way in chunks:
        pl.when(leaves(way, 1))(lambda j=j, way=way: hop(j, way, 1).start())
    if near == 2:
        for j in range(local_toks):
            swap(j, z).start()
    y_ref[tok, smp] = x_ref[smp]
    for copy in copies:
        copy.wait()
    copies = send_all("tok", n_tok, lambda p: y_ref.at[tok], y_ref.at[tok], send_b, recv_b)

    def relay(step, carry):
        for j, way in chunks:

            @pl.when(lands(way, step))
            def _(j=j, way=way):
                arrived(j, way, step)
                pl.when((step + 1 < far) & leaves(way, step + 1))(lambda: hop(j, way, step + 1).start())
                if near == 2:
                    swap(j, z - step if way == 0 else z + step).start()

        return carry

    lax.fori_loop(1, far, relay, 0)

    def finish(step, carry):
        for j, way in chunks:
            pl.when(leaves(way, step))(lambda j=j, way=way: hop(j, way, step).wait_send())
        return carry

    lax.fori_loop(1, far, finish, 0)
    if near == 2:

        def swapped(position, carry):
            for j in range(local_toks):
                swap(j, position).wait()
            return carry

        lax.fori_loop(0, far, swapped, 0)
    for copy in copies:
        copy.wait()


def grads_kernel(n_tok, n_smp, s_ref, y_ref, landed, total, send_a, recv_a, send_b, recv_b):
    tok, smp = lax.axis_index("tok"), lax.axis_index("smp")
    greet((("smp", n_smp), ("tok", n_tok)))
    copies = send_all("tok", n_tok, lambda p: s_ref.at[p], landed.at[tok], send_a, recv_a)
    landed[tok] = s_ref[tok]
    for copy in copies:
        copy.wait()
    total[...] = jnp.sum(landed[...], axis=0)
    copies = send_all("smp", n_smp, lambda p: total.at[p], y_ref.at[smp], send_b, recv_b)
    y_ref[smp] = total[smp]
    for copy in copies:
        copy.wait()


def logits_kernel(n_tok, x_ref, y_ref, landed, send_sem, recv_sem):
    tok = lax.axis_index("tok")
    greet((("tok", n_tok),))
    copies = send_all("tok", n_tok, lambda p: x_ref, landed.at[tok], send_sem, recv_sem)
    landed[tok] = x_ref[...]
    for copy in copies:
        copy.wait()
    y_ref[...] = jnp.sum(landed[...], axis=0)


def call(kernel, operand, out_shape, scratch, sems, ident):
    return pl.pallas_call(
        kernel,
        out_shape=jax.ShapeDtypeStruct(out_shape, jnp.float32),
        in_specs=[pl.BlockSpec(memory_space=VMEM)],
        out_specs=pl.BlockSpec(memory_space=VMEM),
        scratch_shapes=[VMEM(s, jnp.float32) for s in scratch]
        + [pltpu.SemaphoreType.DMA((n,)) for n in sems],
        compiler_params=pltpu.CompilerParams(
            collective_id=ident, has_side_effects=True, vmem_limit_bytes=24 << 20
        ),
        cost_estimate=pl.CostEstimate(flops=0, bytes_accessed=30_000_000, transcendentals=0),
    )(operand)


def on_device(
    n_tok,
    n_smp,
    row_table,
    row_accum,
    last_step,
    step_now,
    row_ids,
    row_counts,
    sample_slots,
    labels,
    up_weight,
    down_weight,
    out_weight,
):
    highest = lax.Precision.HIGHEST
    local_toks, shard_rows, width = row_table.shape
    groups, capacity = row_ids.shape[2:]
    batch = labels.shape[0]
    toks = sample_slots.shape[0]
    head = width // toks
    rows = local_toks * capacity
    flat = n_tok * n_smp * rows
    tok, smp = lax.axis_index("tok"), lax.axis_index("smp")

    factor = jnp.exp((step_now[0] - last_step).astype(jnp.float32) * decay_log)
    ids = row_ids[:, 0].transpose(1, 0, 2)
    valid = jnp.arange(capacity)[None, None, :] < row_counts[:, 0].T[:, :, None]
    pick = ids[..., None] == jnp.arange(shard_rows)
    looked = jnp.einsum(
        "gjcr,jrd->gjcd", pick.astype(jnp.float32), row_table * factor[:, :, None], precision=highest
    ).reshape(groups, rows, width)
    near = 2 if n_smp % 2 == 0 else 1
    far = n_smp // near
    up_blocks = up_weight.transpose(1, 0, 2)
    hops = (local_toks, 2, far)
    lists, up_full = pl.pallas_call(
        functools.partial(lists_kernel, n_tok, n_smp, near),
        out_shape=(
            jax.ShapeDtypeStruct((n_tok, n_smp, rows, width), jnp.float32),
            jax.ShapeDtypeStruct((local_toks, n_smp) + up_blocks.shape[1:], jnp.bfloat16),
        ),
        in_specs=[pl.BlockSpec(memory_space=VMEM)] * 2,
        out_specs=(pl.BlockSpec(memory_space=VMEM),) * 2,
        scratch_shapes=[pltpu.SemaphoreType.DMA((n,)) for n in (n_smp, n_smp, n_tok, n_tok)]
        + [pltpu.SemaphoreType.DMA(n) for n in (hops, hops, (local_toks, far), (local_toks, far))],
        compiler_params=pltpu.CompilerParams(
            collective_id=1, has_side_effects=True, vmem_limit_bytes=24 << 20
        ),
        cost_estimate=pl.CostEstimate(flops=0, bytes_accessed=60_000_000, transcendentals=0),
    )(looked, up_blocks)
    lists, up_full, down_weight = lax.optimization_barrier((lists, up_full, down_weight))
    down_full = lax.all_gather(down_weight, "smp", axis=0, tiled=True)
    lists = lists.reshape(flat, width)
    up_full = up_full.reshape(local_toks, width, -1)

    place = jnp.arange(n_smp)[:, None] * capacity + jnp.arange(capacity)
    slots = sample_slots.reshape(n_tok, 1, local_toks, 1, batch)
    hits = (slots == place[None, :, None, :, None]).astype(jnp.float32).reshape(flat, batch)
    number = jnp.arange(flat)
    token = number // (n_smp * rows) * local_toks + number % rows // capacity
    block = token[:, None] == (jnp.arange(width) // head)[None, :]
    mine = [(token == tok * local_toks + j)[:, None] for j in range(local_toks)]

    gathered = []
    for j in range(local_toks):
        part = lax.dynamic_slice_in_dim(lists, (tok * local_toks + j) * head, head, 1)
        spread = jnp.where(block, jnp.tile(part, (1, toks)), 0.0)
        gathered.append(spread + jnp.where(mine[j], lists, 0.0))
    summed = jnp.einsum("kb,jkd->jbd", hits, jnp.stack(gathered), precision=highest)
    normed_in, inverse_in = normalize(summed)
    input_bf = normed_in.astype(jnp.bfloat16)
    preact = jnp.einsum("jbd,jdf->jbf", input_bf, up_full, preferred_element_type=jnp.float32)
    active = jax.nn.gelu(preact, approximate=False).astype(jnp.bfloat16)
    output = jnp.einsum("jbf,djf->jbd", active, down_full, preferred_element_type=jnp.float32)
    normed_out, inverse_out = normalize(normed_in + output)
    partial_logit = jnp.sum(normed_out * out_weight[:, None, :], axis=(0, 2))
    logits = call(
        functools.partial(logits_kernel, n_tok),
        partial_logit.reshape(1, batch),
        (1, batch),
        [(n_tok, 1, batch)],
        [n_tok, n_tok],
        2,
    ).reshape(batch)
    dlogit = jax.nn.sigmoid(logits) - labels.astype(jnp.float32)
    grad_sum = norm_back(dlogit[None, :, None] * out_weight[:, None, :], normed_out, inverse_out)
    grad_out_bf = grad_sum.astype(jnp.bfloat16)

    z, core = smp // near, smp % near
    pairs = []
    for j in range(local_toks):
        partial = jnp.einsum("bd,bf->df", grad_out_bf[j], active[j], preferred_element_type=jnp.float32)
        partial = partial.reshape(far, near, width // n_smp, -1)
        pair = lax.dynamic_index_in_dim(partial, core, 1, keepdims=False)
        if near == 2:
            other = lax.dynamic_index_in_dim(partial, 1 - core, 1, keepdims=False)
            pair = pair + lax.ppermute(other, "smp", [(i, i ^ 1) for i in range(n_smp)])
        pairs.append(pair)

    def far_sums(pairs):
        def blocks(position):
            parts = [lax.dynamic_index_in_dim(pair, position, 0, keepdims=False) for pair in pairs]
            return jnp.concatenate(parts, axis=0)

        grad_down = blocks(z)
        flip = far & (far - 1) == 0
        for k in range(far - 1, 0, -1):
            part = blocks(z ^ k if flip else (z + k) % far)
            if not (flip and k == 1):
                part = part.astype(jnp.bfloat16)
            route = [(i, i ^ (k * near) if flip else (i + k * near) % n_smp) for i in range(n_smp)]
            grad_down = grad_down + lax.ppermute(part, "smp", route).astype(jnp.float32)
        return jnp.stack(jnp.split(grad_down, local_toks, axis=0), axis=1)

    grad_active = jnp.einsum(
        "jbd,djf->jbf", grad_out_bf, down_full, preferred_element_type=jnp.float32
    )
    grad_pre = (grad_active * gelu_grad(preact)).astype(jnp.bfloat16)
    grad_normed = grad_sum + jnp.einsum(
        "jbf,jdf->jbd", grad_pre, up_full, preferred_element_type=jnp.float32
    )
    grad_mixed = norm_back(grad_normed, normed_in, inverse_in)
    pairs, grad_mixed = lax.optimization_barrier((pairs, grad_mixed))
    grad_down = far_sums(pairs)

    sums = jnp.einsum("kb,jbd->jkd", hits, grad_mixed, precision=highest)
    sent = jnp.zeros((flat, width), jnp.float32)
    for j in range(local_toks):
        own_head = (jnp.arange(width) // head == tok * local_toks + j)[None, :]
        heads = jnp.where(block, sums[j], 0.0).reshape(flat, toks, head).sum(axis=1)
        sent = sent + jnp.where(own_head, jnp.tile(heads, (1, toks)), 0.0)
        sent = sent + jnp.where(mine[j], sums[j], 0.0)
    back = call(
        functools.partial(grads_kernel, n_tok, n_smp),
        sent.reshape(n_tok, n_smp, rows, width),
        (n_smp, rows, width),
        [(n_tok, n_smp, rows, width), (n_smp, rows, width)],
        [n_tok, n_tok, n_smp, n_smp],
        3,
    ).reshape(groups, local_toks, capacity, width)

    taken = (pick & valid[..., None]).astype(jnp.float32)
    row_grads = jnp.einsum("gjcr,gjcd->jrd", taken, back, precision=highest)
    touched = jnp.sum(taken, axis=(0, 2)) > 0.0
    new_accum = row_accum + jnp.mean(row_grads * row_grads, axis=2)
    updated = row_table * factor[:, :, None] - learn_rate * row_grads * lax.rsqrt(new_accum)[:, :, None]
    new_table = jnp.where(touched[:, :, None], updated, row_table)
    return (new_table, new_accum, grad_down, logits)


def solution(mesh):
    return jax.shard_map(
        functools.partial(on_device, mesh.shape["tok"], mesh.shape["smp"]),
        mesh=mesh,
        in_specs=(
            P("tok", "smp", None),
            P("tok", "smp"),
            P("tok", "smp"),
            P(),
            P("tok", "smp", None, None),
            P("tok", "smp", None),
            P(None, "smp"),
            P("smp"),
            P("smp", "tok", None),
            P("smp", "tok", None),
            P("tok", None),
        ),
        out_specs=(P("tok", "smp", None), P("tok", "smp"), P("smp", "tok", None), P("smp")),
        check_vma=False,
    )
```
